32 devices in a mesh: dp: 2 (over y), section: 4 (over x, core), mp: 4 (over z).
Axes of the slice: x: 2, y: 2, z: 4, core: 2. Of those that a mesh axis runs over, the one named last changes fastest.
Arguments:
- hidden_in: bfloat16 [4, 128, 4096], P('dp')
- slot_hidden: bfloat16 [4, 4, 16, 4096], P('section', 'dp'), may hold values from -6 to 6
- norm_gain: float32 [4, 4096], P('section'), may hold values from 0.5 to 1.5
- w_query: bfloat16 [4, 4096, 3072], P('section', None, 'mp')
- w_key: bfloat16 [4, 4096, 1024], P('section', None, 'mp')
- w_value: bfloat16 [4, 4096, 1024], P('section', None, 'mp'), may hold values from -0.09375 to 0.09375
- w_out: bfloat16 [4, 3072, 4096], P('section', 'mp'), may hold values from -0.109375 to 0.109375
- key_a: bfloat16 [4, 4096, 64], P('section'), may hold values from -0.09375 to 0.09375
- key_b: bfloat16 [4, 64, 1024], P('section', None, 'mp'), may hold values from -0.375 to 0.375
- value_a: bfloat16 [4, 4096, 64], P('section'), may hold values from -0.09375 to 0.09375
- value_b: bfloat16 [4, 64, 1024], P('section', None, 'mp'), may hold values from -0.375 to 0.375
- cotangent: bfloat16 [4, 128, 4096], P('dp'), may hold values from -6 to 6
Outputs:
- grad_a: float32 [4, 2, 4096, 64], P('section')
- grad_b: float32 [4, 2, 64, 1024], P('section', None, None, 'mp')
The draws below stay inside these ranges and needn't reach their ends.
All inputs are finite; a program needn't handle non-finite values.
Results may differ from the reference program's by a relative error of at most 0.028.
Values may be sent and summed in bfloat16 or wider, within the bound.
A program may use at most 128 MiB of HBM per device.

```python
import math
import jax
import jax.numpy as jnp
from jax import lax

D = 4096
QH = 24
KVH = 8
HD = 128
SLOTS = 16
RANK = 64
BLOCK = 128
LAYERS = 4
BLOCKS = 4


def key_query(key):
    streams = jax.random.split(jax.random.fold_in(key, 17), 2)
    key_weights = jax.random.normal(streams[0], (LAYERS, D, KVH * HD), jnp.float32) / math.sqrt(D)
    query_weights = jax.random.normal(streams[1], (LAYERS, D, QH * HD), jnp.float32) / math.sqrt(D)
    return (key_weights, query_weights)


def draw_w_key(key, part):
    return key_query(key)[0].astype(jnp.bfloat16)


def draw_w_query(key, part):
    return key_query(key)[1].astype(jnp.bfloat16)


def draw_hidden_in(key, part):
    streams = jax.random.split(jax.random.fold_in(key, 3), 3)
    values = jax.random.normal(streams[0], (BLOCKS, BLOCK, D), jnp.float32)
    scales = jnp.exp(jax.random.uniform(streams[2], (BLOCKS, BLOCK, 1), jnp.float32, 0.0, math.log(10.0)))
    return (values * scales).astype(jnp.bfloat16)


def level_of(rng, extent, shards, least, largest):
    level = 1.0
    for dim, shards_of in shards:
        heights = jax.random.uniform(jax.random.fold_in(jax.random.fold_in(rng, 6), dim), (shards_of,), jnp.float32, least / len(shards), largest / len(shards))
        level = level * jnp.repeat(jnp.exp(heights), extent[dim] // shards_of).reshape((-1,) + (1,) * (len(extent) - 1 - dim))
    return level


def centred(stream_key, shape, deviation, reach, shards=(), kind=jnp.bfloat16):
    drawn = deviation * jax.random.normal(stream_key, shape, jnp.float32)
    if shards:
        drawn = drawn * level_of(stream_key, shape, shards, -0.22, 0.18)
    return jnp.clip(drawn, -reach, reach).astype(kind)


def setup_inputs(seed: int = 0) -> dict:
    splits = jax.random.split(jax.random.key(seed), 13)
    hidden_in = draw_hidden_in(jax.random.fold_in(splits[12], 71), 0)
    slot_hidden = centred(splits[1], (LAYERS, BLOCKS, SLOTS, D), 1.0, 6.0, ((0, 4), (1, 2)))
    norm_gain = jnp.clip(1.0 + 0.1 * jax.random.normal(splits[2], (LAYERS, D), jnp.float32), 0.5, 1.5)
    w_query = draw_w_query(jax.random.fold_in(splits[12], 71), 0)
    w_key = draw_w_key(jax.random.fold_in(splits[12], 71), 0)
    w_value = centred(splits[5], (LAYERS, D, KVH * HD), D ** -0.5, 0.09375, ((0, 4), (2, 4)))
    w_out = centred(splits[6], (LAYERS, QH * HD, D), (QH * HD) ** -0.5, 0.109375, ((0, 4), (1, 4)))
    key_a = centred(splits[7], (LAYERS, D, RANK), D ** -0.5, 0.09375, ((0, 4),))
    key_b = centred(splits[8], (LAYERS, RANK, KVH * HD), (4 * RANK) ** -0.5, 0.375, ((0, 4), (2, 4)))
    value_a = centred(splits[9], (LAYERS, D, RANK), D ** -0.5, 0.09375, ((0, 4),))
    value_b = centred(splits[10], (LAYERS, RANK, KVH * HD), (4 * RANK) ** -0.5, 0.375, ((0, 4), (2, 4)))
    cotangent = centred(splits[11], (BLOCKS, BLOCK, D), 1.0, 6.0, ((0, 2),))
    return dict(hidden_in=hidden_in, slot_hidden=slot_hidden, norm_gain=norm_gain, w_query=w_query, w_key=w_key, w_value=w_value, w_out=w_out, key_a=key_a, key_b=key_b, value_a=value_a, value_b=value_b, cotangent=cotangent)


EPS = 1e-05
NEG = -1e+30
HIGH = lax.Precision.HIGHEST

def normalize(rows):
    wide = rows.astype(jnp.float32)
    inverse = lax.rsqrt(lax.optimization_barrier(jnp.mean(wide * wide, axis=-1, keepdims=True)) + EPS)
    return (wide * inverse, inverse)

def visible(count, slots):
    qpos = lax.broadcasted_iota(jnp.int32, (count, slots + count), 0)
    kpos = lax.broadcasted_iota(jnp.int32, (count, slots + count), 1)
    return (kpos < slots) | (kpos - slots <= qpos)

def mixdot(left, right):
    return jnp.dot(left, right, preferred_element_type=jnp.float32)

def attend(query, keys, values):
    query, keys, values = lax.optimization_barrier((query, keys, values))
    count = query.shape[0]
    groups = keys.shape[1] // HD
    per_group = query.shape[1] // keys.shape[1]
    q_four = query.astype(jnp.float32).reshape(count, groups, per_group, HD)
    k_three = keys.astype(jnp.float32).reshape(-1, groups, HD)
    v_three = values.astype(jnp.float32).reshape(-1, groups, HD)
    scores = jnp.einsum('igcd,jgd->gcij', q_four, k_three, precision=HIGH) / math.sqrt(HD)
    scores = jnp.where(visible(count, SLOTS), scores, NEG)
    top = lax.optimization_barrier(jnp.max(scores, axis=-1, keepdims=True))
    probs = jnp.exp(scores - top)
    probs = probs / lax.optimization_barrier(jnp.sum(probs, axis=-1, keepdims=True))
    weights = lax.optimization_barrier(probs.astype(jnp.bfloat16))
    mixed = jnp.einsum('gcij,jgd->igcd', weights.astype(jnp.float32), v_three, precision=HIGH)
    return (mixed.reshape(count, -1).astype(jnp.bfloat16), probs, weights)

def attend_back(grad_mixed, query, keys, values, probs, weights):
    grad_mixed, query, keys, values, weights = lax.optimization_barrier((grad_mixed, query, keys, values, weights))
    count = query.shape[0]
    groups = keys.shape[1] // HD
    per_group = query.shape[1] // keys.shape[1]
    q_four = query.astype(jnp.float32).reshape(count, groups, per_group, HD)
    k_three = keys.astype(jnp.float32).reshape(-1, groups, HD)
    v_three = values.astype(jnp.float32).reshape(-1, groups, HD)
    g_four = grad_mixed.astype(jnp.float32).reshape(count, groups, per_group, HD)
    grad_probs = jnp.einsum('igcd,jgd->gcij', g_four, v_three, precision=HIGH)
    grad_values = jnp.einsum('gcij,igcd->jgd', weights.astype(jnp.float32), g_four, precision=HIGH)
    grad_scores = probs * (grad_probs - lax.optimization_barrier(jnp.sum(probs * grad_probs, axis=-1, keepdims=True)))
    scaled = lax.optimization_barrier((grad_scores / math.sqrt(HD)).astype(jnp.bfloat16))
    grad_query = jnp.einsum('gcij,jgd->igcd', scaled.astype(jnp.float32), k_three, precision=HIGH)
    grad_keys = jnp.einsum('gcij,igcd->jgd', scaled.astype(jnp.float32), q_four, precision=HIGH)
    return (grad_query.reshape(count, -1).astype(jnp.bfloat16), grad_keys.reshape(-1, groups * HD), grad_values.reshape(-1, groups * HD))

def slot_entries(slot_rows, gain, w_key, w_value, key_a, key_b, value_a, value_b):
    unit, inverse = normalize(slot_rows)
    slot_normed = lax.optimization_barrier((unit * gain).astype(jnp.bfloat16))
    low_key = mixdot(slot_normed, key_a).astype(jnp.bfloat16)
    low_value = mixdot(slot_normed, value_a).astype(jnp.bfloat16)
    slot_keys = (mixdot(slot_normed, w_key) + mixdot(low_key, key_b)).astype(jnp.bfloat16)
    slot_values = (mixdot(slot_normed, w_value) + mixdot(low_value, value_b)).astype(jnp.bfloat16)
    return (slot_normed, low_key, low_value, slot_keys, slot_values)

def layer_core(rows, slot_rows, params):
    gain, w_query, w_key, w_value, w_out, key_a, key_b, value_a, value_b = params
    unit, inverse = normalize(rows)
    normed = (unit * gain).astype(jnp.bfloat16)
    query = mixdot(normed, w_query).astype(jnp.bfloat16)
    key_tok = mixdot(normed, w_key).astype(jnp.bfloat16)
    value_tok = mixdot(normed, w_value).astype(jnp.bfloat16)
    slot_normed, low_key, low_value, slot_keys, slot_values = slot_entries(slot_rows, gain, w_key, w_value, key_a, key_b, value_a, value_b)
    keys = jnp.concatenate([slot_keys, key_tok], axis=0)
    values = jnp.concatenate([slot_values, value_tok], axis=0)
    mixed, probs, weights = attend(query, keys, values)
    return (unit, inverse, query, keys, values, mixed, probs, weights, slot_normed, low_key, low_value)

def forward(rows, slot_rows, params):
    mixed = layer_core(rows, slot_rows, params)[5]
    return (rows.astype(jnp.float32) + mixdot(mixed, params[4])).astype(jnp.bfloat16)

def backward(rows, slot_rows, grad, params):
    gain, w_query, w_key, w_value, w_out, key_a, key_b, value_a, value_b = params
    unit, inverse, query, keys, values, mixed, probs, weights, slot_normed, low_key, low_value = layer_core(rows, slot_rows, params)
    grad_low = grad.astype(jnp.bfloat16)
    grad_mixed = mixdot(grad_low, w_out.T).astype(jnp.bfloat16)
    grad_query, grad_keys, grad_values = attend_back(grad_mixed, query, keys, values, probs, weights)
    key_grad = grad_keys.astype(jnp.bfloat16)
    value_grad = grad_values.astype(jnp.bfloat16)
    grad_normed = mixdot(grad_query, w_query.T) + mixdot(key_grad[SLOTS:], w_key.T) + mixdot(value_grad[SLOTS:], w_value.T)
    scaled = grad_normed * gain
    grad_rows = grad + inverse * (scaled - unit * lax.optimization_barrier(jnp.mean(scaled * unit, axis=-1, keepdims=True)))
    slot_key_grad = key_grad[:SLOTS]
    slot_value_grad = value_grad[:SLOTS]
    grad_b = jnp.stack([mixdot(low_key.T, slot_key_grad), mixdot(low_value.T, slot_value_grad)])
    low_grads = jnp.stack([mixdot(slot_key_grad, key_b.T), mixdot(slot_value_grad, value_b.T)])
    grad_a = jnp.einsum('sd,tsr->tdr', slot_normed.astype(jnp.float32), low_grads, precision=HIGH)
    return (grad_rows, grad_a, grad_b)

def reference(hidden_in, slot_hidden, norm_gain, w_query, w_key, w_value, w_out, key_a, key_b, value_a, value_b, cotangent):

    def params(layer):
        return (norm_gain[layer], w_query[layer], w_key[layer], w_value[layer], w_out[layer], key_a[layer], key_b[layer], value_a[layer], value_b[layer])

    def one_block(totals, block):
        rows, slot_rows, grad_out = block
        inputs = []
        current = rows
        for layer in range(LAYERS):
            inputs.append(current)
            if layer + 1 < LAYERS:
                current = forward(current, slot_rows[layer], params(layer))
        grad = grad_out.astype(jnp.float32)
        parts_a = [None] * LAYERS
        parts_b = [None] * LAYERS
        for layer in reversed(range(LAYERS)):
            grad, part_a, part_b = backward(inputs[layer], slot_rows[layer], grad, params(layer))
            parts_a[layer] = part_a
            parts_b[layer] = part_b
        return ((totals[0] + jnp.stack(parts_a), totals[1] + jnp.stack(parts_b)), None)
    start = (jnp.zeros((LAYERS, 2, D, RANK), jnp.float32), jnp.zeros((LAYERS, 2, RANK, KVH * HD), jnp.float32))
    slots_by_block = jnp.swapaxes(slot_hidden, 0, 1)
    totals, unused = lax.scan(one_block, start, (hidden_in, slots_by_block, cotangent))
    return (totals[0], totals[1])
```

```python
import functools
import math

import jax
import jax.numpy as jnp
from jax import lax
from jax.experimental import pallas as pl
from jax.experimental.pallas import tpu as pltpu
from jax.sharding import PartitionSpec as P

HD = 128
EPS = 1e-05
NEG = -1e30
HIGH = lax.Precision.HIGHEST
MESH = pl.DeviceIdType.MESH
CHUNKS = 4
F32 = jnp.float32
BF16 = jnp.bfloat16


def dot(a, b):
    return jnp.dot(a, b, preferred_element_type=F32)


def dot_nt(a, b):
    return lax.dot_general(a, b, (((1,), (1,)), ((), ())), preferred_element_type=F32)


def dot_tn(a, b):
    return lax.dot_general(a, b, (((0,), (0,)), ((), ())), preferred_element_type=F32)


def kernel(
    ndp,
    nsec,
    nmp,
    hidden,
    slots,
    gain,
    w_q,
    w_k,
    w_v,
    w_out,
    key_a,
    key_b,
    value_a,
    value_b,
    cot,
    sn_out,
    low_out,
    low_total_out,
    ks_out,
    w_all,
    w_o,
    rows,
    grads,
    xn,
    part_f,
    part_b,
    rs_f,
    rs_b,
    own_f,
    own_b,
    q,
    kpad,
    vpad,
    probs,
    mixed,
    gmix,
    dqkv,
    sn_all,
    low_all,
    lg_all,
    ks_all,
    w_sem,
    in_sem,
    rsf_s,
    rsf_r,
    rsb_s,
    rsb_r,
    agf_s,
    agf_r,
    agb_s,
    agb_r,
    sn_s,
    sn_r,
    lo_s,
    lo_r,
    lg_s,
    lg_r,
    ks_s,
    ks_r,
):
    dp = lax.axis_index("dp")
    sec = lax.axis_index("section")
    mp = lax.axis_index("mp")
    last = nsec - 1
    nb, count, width = rows.shape
    ns = slots.shape[1] // nb
    share = count // nmp
    ch = width // CHUNKS
    qw = q.shape[2]
    kw = kpad.shape[2]
    groups = kw // HD
    per = qw // kw
    padded = kpad.shape[1]
    scale = 1.0 / math.sqrt(HD)

    loads = [
        pltpu.make_async_copy(w_k.at[0], w_all.at[:, pl.ds(qw, kw)], w_sem.at[0]),
        pltpu.make_async_copy(w_v.at[0], w_all.at[:, pl.ds(qw + kw, kw)], w_sem.at[1]),
        pltpu.make_async_copy(w_q.at[0], w_all.at[:, pl.ds(0, qw)], w_sem.at[2]),
        pltpu.make_async_copy(w_out.at[0], w_o, w_sem.at[3]),
    ]
    for load in loads:
        load.start()
    load_rows = pltpu.make_async_copy(hidden, rows, in_sem.at[0])
    load_cot = pltpu.make_async_copy(cot, grads, in_sem.at[1])

    @pl.when(sec == 0)
    def _():
        load_rows.start()

    @pl.when(sec == last)
    def _():
        load_cot.start()

    bar = pltpu.get_barrier_semaphore()
    for a in range(ndp):
        for b in range(nmp):
            if a or b:
                pl.semaphore_signal(
                    bar,
                    inc=1,
                    device_id={"dp": lax.rem(dp + a, ndp), "mp": lax.rem(mp + b, nmp)},
                    device_id_type=MESH,
                )

    @pl.when(sec < last)
    def _():
        for b in range(nmp):
            pl.semaphore_signal(
                bar, inc=1, device_id={"section": sec + 1, "mp": b}, device_id_type=MESH
            )

    @pl.when(sec > 0)
    def _():
        for b in range(nmp):
            pl.semaphore_signal(
                bar, inc=1, device_id={"section": sec - 1, "mp": b}, device_id_type=MESH
            )

    edge = jnp.where((sec == 0) | (sec == last), nmp, 2 * nmp)
    pl.semaphore_wait(bar, ndp * nmp - 1 + edge)

    def dp_copy(buf, send, recv, a, source):
        return pltpu.make_async_remote_copy(
            src_ref=buf.at[source],
            dst_ref=buf.at[source],
            send_sem=send.at[a - 1],
            recv_sem=recv.at[a - 1],
            device_id={"dp": lax.rem(dp + a, ndp)},
            device_id_type=MESH,
        )

    def dp_send(buf, send, recv):
        for a in range(1, ndp):
            dp_copy(buf, send, recv, a, dp).start()

    def dp_wait(buf, send, recv):
        for a in range(1, ndp):
            dp_copy(buf, send, recv, a, lax.rem(dp - a + ndp, ndp)).wait_recv()
        for a in range(1, ndp):
            dp_copy(buf, send, recv, a, dp).wait_send()

    wide = slots[0].astype(F32)
    inverse = lax.rsqrt(jnp.mean(wide * wide, axis=-1, keepdims=True) + EPS)
    sn_all[dp] = (wide * inverse * gain[...]).astype(BF16)
    dp_send(sn_all, sn_s, sn_r)
    sn = sn_all[dp]
    low_k = dot(sn, key_a[0]).astype(BF16)
    low_v = dot(sn, value_a[0]).astype(BF16)
    low_all[dp, 0] = low_k
    low_all[dp, 1] = low_v
    dp_send(low_all, lo_s, lo_r)
    loads[0].wait()
    slot_k = (dot(sn, w_all[:, qw : qw + kw]) + dot(low_k, key_b[0])).astype(BF16)
    loads[1].wait()
    slot_v = (dot(sn, w_all[:, qw + kw : qw + 2 * kw]) + dot(low_v, value_b[0])).astype(BF16)
    kpad[...] = jnp.zeros_like(kpad)
    vpad[...] = jnp.zeros_like(vpad)
    for m in range(nb):
        kpad[m, count : count + ns, :] = slot_k[m * ns : (m + 1) * ns]
        vpad[m, count : count + ns, :] = slot_v[m * ns : (m + 1) * ns]
    loads[2].wait()
    loads[3].wait()

    @pl.when(sec == 0)
    def _():
        load_rows.wait()

    @pl.when(sec == last)
    def _():
        load_cot.wait()

    def cols(c):
        return pl.ds(pl.multiple_of(c * ch, ch), ch)

    def share_rows(j):
        return pl.ds(pl.multiple_of(j * share, share), share)

    def sem_at(m, c, j):
        return (m * CHUNKS + c) * nmp + j

    def rs_copy(part, land, send, recv, m, c, to, source):
        return pltpu.make_async_remote_copy(
            src_ref=part.at[m, share_rows(to), cols(c)],
            dst_ref=land.at[m, source, :, cols(c)],
            send_sem=send.at[sem_at(m, c, to)],
            recv_sem=recv.at[sem_at(m, c, source)],
            device_id={"mp": to},
            device_id_type=MESH,
        )

    def ag_copy(own, land, send, recv, m, c, to, source, section):
        return pltpu.make_async_remote_copy(
            src_ref=own.at[m, :, cols(c)],
            dst_ref=land.at[m, share_rows(source), cols(c)],
            send_sem=send.at[sem_at(m, c, to)],
            recv_sem=recv.at[sem_at(m, c, source)],
            device_id={"section": section, "mp": to},
            device_id_type=MESH,
        )

    def peer(d):
        return lax.rem(mp + d, nmp)

    def rs_send(part, land, send, recv, m, c):
        for d in range(1, nmp):
            rs_copy(part, land, send, recv, m, c, peer(d), mp).start()

    def rs_wait(part, land, send, recv, m, c):
        for d in range(1, nmp):
            rs_copy(part, land, send, recv, m, c, peer(d), peer(d)).wait_recv()

    def ag_send(own, land, send, recv, m, c, section):
        for d in range(nmp):
            ag_copy(own, land, send, recv, m, c, peer(d), mp, section).start()

    def ag_wait(own, land, send, recv, m, section):
        @pl.loop(0, CHUNKS)
        def _(c):
            for j in range(nmp):
                ag_copy(own, land, send, recv, m, c, j, j, section).wait_recv()

    def rs_total(part, land, m, c):
        total = part[m, share_rows(mp), cols(c)].astype(F32)
        for d in range(1, nmp):
            total = total + land[m, peer(d), :, cols(c)].astype(F32)
        return total

    def stacked(ref, lead, g):
        parts = []
        for h in range(per):
            low = (g * per + h) * HD
            if lead is None:
                parts.append(ref[:, low : low + HD])
            else:
                parts.append(ref[lead, :, low : low + HD])
        return jnp.concatenate(parts, axis=0)

    def forward(m):
        @pl.when(sec > 0)
        def _():
            ag_wait(own_f, rows, agf_s, agf_r, m, sec - 1)

        @pl.loop(0, count // 16)
        def _(i):
            at = pl.ds(pl.multiple_of(i * 16, 16), 16)
            x = rows[m, at, :].astype(F32)
            inv = lax.rsqrt(jnp.mean(x * x, axis=-1, keepdims=True) + EPS)
            xn[at, :] = (x * inv * gain[...]).astype(BF16)

        @pl.loop(0, per)
        def _(i):
            at = pl.ds(pl.multiple_of(i * kw, kw), kw)
            q[m, :, at] = dot(xn[...], w_all[:, at]).astype(BF16)

        kpad[m, 0:count, :] = dot(xn[...], w_all[:, qw : qw + kw]).astype(BF16)
        vpad[m, 0:count, :] = dot(xn[...], w_all[:, qw + kw : qw + 2 * kw]).astype(BF16)
        i_at = lax.rem(lax.broadcasted_iota(jnp.int32, (per * count, padded), 0), count)
        j_at = lax.broadcasted_iota(jnp.int32, (per * count, padded), 1)
        seen = (j_at <= i_at) | ((j_at >= count) & (j_at < count + ns))
        for g in range(groups):
            gc = slice(g * HD, (g + 1) * HD)
            scores = dot_nt(stacked(q, m, g), kpad[m, :, gc]) * scale
            scores = jnp.where(seen, scores, NEG)
            e = jnp.exp(scores - jnp.max(scores, axis=-1, keepdims=True))
            p = e / jnp.sum(e, axis=-1, keepdims=True)
            probs[m, g] = p
            o = dot(p.astype(BF16), vpad[m, :, gc]).astype(BF16)
            for h in range(per):
                low = (g * per + h) * HD
                mixed[:, low : low + HD] = o[h * count : (h + 1) * count]

        @pl.when(sec < last)
        def _():
            @pl.loop(0, CHUNKS)
            def _(c):
                part_f[m, :, cols(c)] = dot(mixed[...], w_o[:, cols(c)]).astype(BF16)
                rs_send(part_f, rs_f, rsf_s, rsf_r, m, c)

    def forward_reduce(m):
        @pl.loop(0, CHUNKS)
        def _(c):
            rs_wait(part_f, rs_f, rsf_s, rsf_r, m, c)
            total = rs_total(part_f, rs_f, m, c)
            total = total + rows[m, share_rows(mp), cols(c)].astype(F32)
            own_f[m, :, cols(c)] = total.astype(BF16)
            ag_send(own_f, rows, agf_s, agf_r, m, c, sec + 1)

    def backward(m):
        @pl.when(sec < last)
        def _():
            ag_wait(own_b, grads, agb_s, agb_r, m, sec + 1)

        @pl.loop(0, per)
        def _(i):
            at = pl.ds(pl.multiple_of(i * kw, kw), kw)
            gmix[:, at] = dot_nt(grads[m], w_o[at, :]).astype(BF16)

        at_slot = pl.ds(pl.multiple_of(m * ns, ns), ns)
        for g in range(groups):
            gc = slice(g * HD, (g + 1) * HD)
            gm = stacked(gmix, None, g)
            p = probs[m, g]
            kg = kpad[m, :, gc]
            gp = dot_nt(gm, vpad[m, :, gc])
            gv = dot_tn(p.astype(BF16), gm).astype(BF16)
            gs = p * (gp - jnp.sum(p * gp, axis=-1, keepdims=True))
            gs = (gs * scale).astype(BF16)
            gq = dot(gs, kg).astype(BF16)
            gk = dot_tn(gs, stacked(q, m, g)).astype(BF16)
            for h in range(per):
                low = (g * per + h) * HD
                dqkv[:, low : low + HD] = gq[h * count : (h + 1) * count]
            dqkv[:, qw + g * HD : qw + (g + 1) * HD] = gk[:count]
            dqkv[:, qw + kw + g * HD : qw + kw + (g + 1) * HD] = gv[:count]
            ks_all[dp, 0, at_slot, gc] = gk[count : count + ns]
            ks_all[dp, 1, at_slot, gc] = gv[count : count + ns]

        @pl.when(sec > 0)
        def _():
            @pl.loop(0, CHUNKS)
            def _(c):
                part_b[m, :, cols(c)] = dot_nt(dqkv[...], w_all[cols(c), :]).astype(BF16)
                rs_send(part_b, rs_b, rsb_s, rsb_r, m, c)

    def backward_reduce(m):
        @pl.loop(0, CHUNKS)
        def _(c):
            rs_wait(part_b, rs_b, rsb_s, rsb_r, m, c)

        mine = share_rows(mp)
        x = rows[m, mine, :].astype(F32)
        inv = lax.rsqrt(jnp.mean(x * x, axis=-1, keepdims=True) + EPS)
        unit = x * inv
        total = part_b[m, mine, :].astype(F32)
        for d in range(1, nmp):
            total = total + rs_b[m, peer(d)].astype(F32)
        scaled = total * gain[...]
        mean = jnp.mean(scaled * unit, axis=-1, keepdims=True)
        own_b[m] = (grads[m, mine, :].astype(F32) + inv * (scaled - unit * mean)).astype(BF16)

        @pl.loop(0, CHUNKS)
        def _(c):
            ag_send(own_b, grads, agb_s, agb_r, m, c, sec - 1)

    back_at = jnp.where(sec == last, 0, nb)

    @pl.loop(0, 2 * nb + 1)
    def _(t):
        @pl.when(t < nb)
        def _():
            forward(t)

        @pl.when((sec < last) & (t >= 1) & (t < nb + 1))
        def _():
            forward_reduce(t - 1)

        @pl.when((t >= back_at) & (t < back_at + nb))
        def _():
            backward(t - back_at)

        @pl.when((sec > 0) & (t >= back_at + 1) & (t < back_at + nb + 1))
        def _():
            backward_reduce(t - back_at - 1)

    dp_send(ks_all, ks_s, ks_r)
    me = dp * nmp + mp
    lg_all[me, 0] = dot_nt(ks_all[dp, 0], key_b[0])
    lg_all[me, 1] = dot_nt(ks_all[dp, 1], value_b[0])

    def lg_copy(a, b, source):
        return pltpu.make_async_remote_copy(
            src_ref=lg_all.at[source],
            dst_ref=lg_all.at[source],
            send_sem=lg_s.at[a * nmp + b],
            recv_sem=lg_r.at[a * nmp + b],
            device_id={"dp": lax.rem(dp + a, ndp), "mp": lax.rem(mp + b, nmp)},
            device_id_type=MESH,
        )

    others = [(a, b) for a in range(ndp) for b in range(nmp) if a or b]
    for a, b in others:
        lg_copy(a, b, me).start()
    dp_wait(sn_all, sn_s, sn_r)
    dp_wait(low_all, lo_s, lo_r)
    sn_out[...] = sn_all[...]
    low_out[...] = low_all[...]
    dp_wait(ks_all, ks_s, ks_r)
    ks_out[...] = ks_all[...]
    for a, b in others:
        source = lax.rem(dp - a + ndp, ndp) * nmp + lax.rem(mp - b + nmp, nmp)
        lg_copy(a, b, source).wait_recv()
    for a in range(ndp):
        total = lg_all[a * nmp]
        for b in range(1, nmp):
            total = total + lg_all[a * nmp + b]
        low_total_out[a] = total
    for a, b in others:
        lg_copy(a, b, me).wait_send()

    @pl.when(sec < last)
    def _():
        @pl.loop(0, nb * CHUNKS)
        def _(i):
            m, c = i // CHUNKS, lax.rem(i, CHUNKS)
            for d in range(1, nmp):
                rs_copy(part_f, rs_f, rsf_s, rsf_r, m, c, peer(d), mp).wait_send()
            for d in range(nmp):
                ag_copy(own_f, rows, agf_s, agf_r, m, c, peer(d), mp, sec + 1).wait_send()

    @pl.when(sec > 0)
    def _():
        @pl.loop(0, nb * CHUNKS)
        def _(i):
            m, c = i // CHUNKS, lax.rem(i, CHUNKS)
            for d in range(1, nmp):
                rs_copy(part_b, rs_b, rsb_s, rsb_r, m, c, peer(d), mp).wait_send()
            for d in range(nmp):
                ag_copy(own_b, grads, agb_s, agb_r, m, c, peer(d), mp, sec - 1).wait_send()


def local(ndp, nsec, nmp, hidden_in, slot_hidden, norm_gain, w_query, w_key, w_value, w_out,
          key_a, key_b, value_a, value_b, cotangent):
    nb, count, width = hidden_in.shape
    ns = slot_hidden.shape[2]
    qw, kw = w_query.shape[2], w_key.shape[2]
    rank = key_a.shape[2]
    share = count // nmp
    groups = kw // HD
    per = qw // kw
    padded = -(-(count + ns) // 256) * 256
    total_slots = nb * ns
    slots = slot_hidden.reshape(1, total_slots, width)
    vmem = pl.BlockSpec(memory_space=pltpu.VMEM)
    hbm = pl.BlockSpec(memory_space=pl.ANY)
    dma = pltpu.SemaphoreType.DMA
    many = dma((nb * CHUNKS * nmp,))
    few = dma((max(ndp - 1, 1),))
    sn_shape = (ndp, total_slots, width)
    low_shape = (ndp, 2, total_slots, rank)
    ks_shape = (ndp, 2, total_slots, kw)
    sn_all, low_all, low_total, ks_all = pl.pallas_call(
        functools.partial(kernel, ndp, nsec, nmp),
        out_shape=(
            jax.ShapeDtypeStruct(sn_shape, BF16),
            jax.ShapeDtypeStruct(low_shape, BF16),
            jax.ShapeDtypeStruct(low_shape, F32),
            jax.ShapeDtypeStruct(ks_shape, BF16),
        ),
        in_specs=[hbm, vmem, vmem, hbm, hbm, hbm, hbm, vmem, vmem, vmem, vmem, hbm],
        out_specs=(vmem, vmem, vmem, vmem),
        scratch_shapes=[
            pltpu.VMEM((width, qw + 2 * kw), BF16),
            pltpu.VMEM((qw, width), BF16),
            pltpu.VMEM((nb, count, width), BF16),
            pltpu.VMEM((nb, count, width), BF16),
            pltpu.VMEM((count, width), BF16),
            pltpu.VMEM((nb, count, width), BF16),
            pltpu.VMEM((nb, count, width), BF16),
            pltpu.VMEM((nb, nmp, share, width), BF16),
            pltpu.VMEM((nb, nmp, share, width), BF16),
            pltpu.VMEM((nb, share, width), BF16),
            pltpu.VMEM((nb, share, width), BF16),
            pltpu.VMEM((nb, count, qw), BF16),
            pltpu.VMEM((nb, padded, kw), BF16),
            pltpu.VMEM((nb, padded, kw), BF16),
            pltpu.VMEM((nb, groups, per * count, padded), F32),
            pltpu.VMEM((count, qw), BF16),
            pltpu.VMEM((count, qw), BF16),
            pltpu.VMEM((count, qw + 2 * kw), BF16),
            pltpu.VMEM(sn_shape, BF16),
            pltpu.VMEM(low_shape, BF16),
            pltpu.VMEM((ndp * nmp, 2, total_slots, rank), F32),
            pltpu.VMEM(ks_shape, BF16),
            dma((4,)),
            dma((2,)),
            many, many, many, many, many, many, many, many,
            few, few, few, few,
            dma((ndp * nmp,)), dma((ndp * nmp,)),
            few, few,
        ],
        compiler_params=pltpu.CompilerParams(
            collective_id=0, has_side_effects=True, vmem_limit_bytes=58 * 1024 * 1024
        ),
    )(hidden_in, slots, norm_gain, w_query, w_key, w_value, w_out, key_a, key_b, value_a, value_b,
      cotangent)
    grad_a = jnp.einsum("psd,ptsr->tdr", sn_all.astype(F32), low_total, precision=HIGH)
    grad_b = jnp.einsum("ptsr,ptsc->trc", low_all, ks_all, preferred_element_type=F32)
    return (grad_a[None], grad_b[None])


def solution(mesh):
    placed = (
        P("dp", None, None),
        P("section", "dp", None, None),
        P("section", None),
        P("section", None, "mp"),
        P("section", None, "mp"),
        P("section", None, "mp"),
        P("section", "mp", None),
        P("section", None, None),
        P("section", None, "mp"),
        P("section", None, None),
        P("section", None, "mp"),
        P("dp", None, None),
    )
    return jax.shard_map(
        functools.partial(local, mesh.shape["dp"], mesh.shape["section"], mesh.shape["mp"]),
        mesh=mesh,
        in_specs=placed,
        out_specs=(P("section", None, None, None), P("section", None, None, "mp")),
        check_vma=False,
    )
```

```python
import functools
import math

import jax
import jax.numpy as jnp
from jax import lax
from jax.experimental import pallas as pl
from jax.experimental.pallas import tpu as pltpu
from jax.sharding import PartitionSpec as P

HD = 128
EPS = 1e-05
NEG = -1e30
HIGH = lax.Precision.HIGHEST
MESH = pl.DeviceIdType.MESH
CHUNKS = 4
F32 = jnp.float32
BF16 = jnp.bfloat16


def dot(a, b):
    return jnp.dot(a, b, preferred_element_type=F32)


def dot_nt(a, b):
    return lax.dot_general(a, b, (((1,), (1,)), ((), ())), preferred_element_type=F32)


def dot_tn(a, b):
    return lax.dot_general(a, b, (((0,), (0,)), ((), ())), preferred_element_type=F32)


def kernel(
    ndp,
    nsec,
    nmp,
    hidden,
    slots,
    gain,
    w_q,
    w_k,
    w_v,
    w_out,
    key_a,
    key_b,
    value_a,
    value_b,
    cot,
    sn_out,
    low_out,
    low_total_out,
    ks_out,
    w_all,
    w_o,
    rows,
    grads,
    xn,
    part_f,
    part_b,
    rs_f,
    rs_b,
    own_f,
    own_b,
    q,
    kpad,
    vpad,
    probs,
    inv_all,
    mixed,
    gmix,
    dqkv,
    sn_all,
    low_all,
    lg_all,
    ks_all,
    w_sem,
    in_sem,
    rsf_s,
    rsf_r,
    rsb_s,
    rsb_r,
    agf_s,
    agf_r,
    agb_s,
    agb_r,
    sn_s,
    sn_r,
    lo_s,
    lo_r,
    lg_s,
    lg_r,
    ks_s,
    ks_r,
):
    dp = lax.axis_index("dp")
    sec = lax.axis_index("section")
    mp = lax.axis_index("mp")
    last = nsec - 1
    half = nsec // 2
    mate = lax.rem(sec + half, nsec)
    nb, count, width = rows.shape
    ns = slots.shape[1] // nb
    share = count // nmp
    ch = width // CHUNKS
    qw = q.shape[2]
    kw = kpad.shape[2]
    groups = kw // HD
    per = qw // kw
    padded = kpad.shape[1]
    scale = 1.0 / math.sqrt(HD)

    loads = [
        pltpu.make_async_copy(w_k.at[0], w_all.at[:, pl.ds(qw, kw)], w_sem.at[0]),
        pltpu.make_async_copy(w_v.at[0], w_all.at[:, pl.ds(qw + kw, kw)], w_sem.at[1]),
        pltpu.make_async_copy(w_q.at[0], w_all.at[:, pl.ds(0, qw)], w_sem.at[2]),
        pltpu.make_async_copy(w_out.at[0], w_o, w_sem.at[3]),
    ]
    for load in loads:
        load.start()
    load_rows = pltpu.make_async_copy(hidden, rows, in_sem.at[0])
    load_cot = pltpu.make_async_copy(cot, grads, in_sem.at[1])

    @pl.when(sec == 0)
    def _():
        load_rows.start()

    @pl.when(sec == last)
    def _():
        load_cot.start()

    bar = pltpu.get_barrier_semaphore()
    for a in range(nsec):
        for b in range(nmp):
            if a or b:
                pl.semaphore_signal(
                    bar,
                    inc=1,
                    device_id={"section": lax.rem(sec + a, nsec), "mp": lax.rem(mp + b, nmp)},
                    device_id_type=MESH,
                )
    for a in range(1, ndp):
        for b in range(nmp):
            pl.semaphore_signal(
                bar,
                inc=1,
                device_id={"dp": lax.rem(dp + a, ndp), "mp": lax.rem(mp + b, nmp)},
                device_id_type=MESH,
            )
    pl.semaphore_wait(bar, nsec * nmp - 1 + (ndp - 1) * nmp)

    def dp_copy(buf, send, recv, a, source):
        return pltpu.make_async_remote_copy(
            src_ref=buf.at[source],
            dst_ref=buf.at[source],
            send_sem=send.at[a - 1],
            recv_sem=recv.at[a - 1],
            device_id={"dp": lax.rem(dp + a, ndp)},
            device_id_type=MESH,
        )

    def dp_send(buf, send, recv):
        for a in range(1, ndp):
            dp_copy(buf, send, recv, a, dp).start()

    def dp_wait(buf, send, recv):
        for a in range(1, ndp):
            dp_copy(buf, send, recv, a, lax.rem(dp - a + ndp, ndp)).wait_recv()
        for a in range(1, ndp):
            dp_copy(buf, send, recv, a, dp).wait_send()

    wide = slots[0].astype(F32)
    inverse = lax.rsqrt(jnp.mean(wide * wide, axis=-1, keepdims=True) + EPS)
    sn_all[dp] = (wide * inverse * gain[...]).astype(BF16)
    dp_send(sn_all, sn_s, sn_r)
    sn = sn_all[dp]
    low_k = dot_nt(sn, key_a[0]).astype(BF16)
    low_v = dot_nt(sn, value_a[0]).astype(BF16)
    low_all[dp, 0] = low_k
    low_all[dp, 1] = low_v
    dp_send(low_all, lo_s, lo_r)
    loads[0].wait()
    slot_k = (dot(sn, w_all[:, qw : qw + kw]) + dot(low_k, key_b[0])).astype(BF16)
    loads[1].wait()
    slot_v = (dot(sn, w_all[:, qw + kw : qw + 2 * kw]) + dot(low_v, value_b[0])).astype(BF16)
    kpad[...] = jnp.zeros_like(kpad)
    vpad[...] = jnp.zeros_like(vpad)
    for m in range(nb):
        kpad[m, count : count + ns, :] = slot_k[m * ns : (m + 1) * ns]
        vpad[m, count : count + ns, :] = slot_v[m * ns : (m + 1) * ns]
    loads[2].wait()
    loads[3].wait()

    @pl.when(sec == 0)
    def _():
        load_rows.wait()

    @pl.when(sec == last)
    def _():
        load_cot.wait()

    mine = lax.broadcasted_iota(jnp.int32, (count, 1), 0) // share == mp

    def cols(c):
        return pl.ds(pl.multiple_of(c * ch, ch), ch)

    def share_rows(j):
        return pl.ds(pl.multiple_of(j * share, share), share)

    def sem_at(m, c, j):
        return (m * CHUNKS + c) * nmp + j

    def rs_copy(part, land, send, recv, m, c, to, source):
        return pltpu.make_async_remote_copy(
            src_ref=part.at[m, share_rows(to), cols(c)],
            dst_ref=land.at[m, source, :, cols(c)],
            send_sem=send.at[sem_at(m, c, to)],
            recv_sem=recv.at[sem_at(m, c, source)],
            device_id={"section": mate, "mp": to},
            device_id_type=MESH,
        )

    def ag_copy(own, land, send, recv, m, c, to, source, section):
        return pltpu.make_async_remote_copy(
            src_ref=own.at[m, :, cols(c)],
            dst_ref=land.at[m, share_rows(source), cols(c)],
            send_sem=send.at[sem_at(m, c, to)],
            recv_sem=recv.at[sem_at(m, c, source)],
            device_id={"section": section, "mp": to},
            device_id_type=MESH,
        )

    def peer(d):
        return lax.rem(mp + d, nmp)

    def rs_send(part, land, send, recv, m, c):
        for d in range(nmp):
            rs_copy(part, land, send, recv, m, c, peer(d), mp).start()

    def ag_send(own, land, send, recv, m, c, section):
        for d in range(nmp):
            ag_copy(own, land, send, recv, m, c, peer(d), mp, section).start()

    def ag_wait(own, land, send, recv, m, section):
        @pl.loop(0, CHUNKS)
        def _(c):
            for j in range(nmp):
                ag_copy(own, land, send, recv, m, c, j, j, section).wait_recv()

    def reduce(own, part, land, spread, rs_s, rs_r, ag_s, ag_r, m, section):
        @pl.loop(0, CHUNKS)
        def _(c):
            total = None
            for j in range(nmp):
                rs_copy(part, land, rs_s, rs_r, m, c, j, j).wait_recv()
            for j in range(nmp):
                piece = land[m, j, :, cols(c)].astype(F32)
                total = piece if total is None else total + piece
            own[m, :, cols(c)] = total.astype(BF16)
            ag_send(own, spread, ag_s, ag_r, m, c, section)

    def stacked(ref, lead, g):
        parts = []
        for h in range(per):
            low = (g * per + h) * HD
            if lead is None:
                parts.append(ref[:, low : low + HD])
            else:
                parts.append(ref[lead, :, low : low + HD])
        return jnp.concatenate(parts, axis=0)

    def forward(m):
        @pl.when(sec > 0)
        def _():
            ag_wait(own_f, rows, agf_s, agf_r, m, mate)

        @pl.loop(0, count // 16)
        def _(i):
            at = pl.ds(pl.multiple_of(i * 16, 16), 16)
            x = rows[m, at, :].astype(F32)
            inv = lax.rsqrt(jnp.mean(x * x, axis=-1, keepdims=True) + EPS)
            xn[at, :] = (x * inv * gain[...]).astype(BF16)
            inv_all[m, at, :] = jnp.broadcast_to(inv, (16, HD))

        @pl.loop(0, per)
        def _(i):
            at = pl.ds(pl.multiple_of(i * kw, kw), kw)
            q[m, :, at] = dot(xn[...], w_all[:, at]).astype(BF16)

        kpad[m, 0:count, :] = dot(xn[...], w_all[:, qw : qw + kw]).astype(BF16)
        vpad[m, 0:count, :] = dot(xn[...], w_all[:, qw + kw : qw + 2 * kw]).astype(BF16)
        i_at = lax.rem(lax.broadcasted_iota(jnp.int32, (per * count, padded), 0), count)
        j_at = lax.broadcasted_iota(jnp.int32, (per * count, padded), 1)
        seen = (j_at <= i_at) | ((j_at >= count) & (j_at < count + ns))
        for g in range(groups):
            gc = slice(g * HD, (g + 1) * HD)
            scores = dot_nt(stacked(q, m, g), kpad[m, :, gc]) * scale
            scores = jnp.where(seen, scores, NEG)
            e = jnp.exp(scores - jnp.max(scores, axis=-1, keepdims=True))
            p = e / jnp.sum(e, axis=-1, keepdims=True)
            probs[m, g] = p
            o = dot(p.astype(BF16), vpad[m, :, gc]).astype(BF16)
            for h in range(per):
                low = (g * per + h) * HD
                mixed[:, low : low + HD] = o[h * count : (h + 1) * count]

        @pl.when(sec < last)
        def _():
            @pl.loop(0, CHUNKS)
            def _(c):
                term = dot(mixed[...], w_o[:, cols(c)])
                term = term + jnp.where(mine, rows[m, :, cols(c)].astype(F32), 0.0)
                part_f[m, :, cols(c)] = term.astype(BF16)
                rs_send(part_f, rs_f, rsf_s, rsf_r, m, c)

    def backward(m):
        @pl.when(sec < last)
        def _():
            ag_wait(own_b, grads, agb_s, agb_r, m, mate)

        @pl.loop(0, per)
        def _(i):
            at = pl.ds(pl.multiple_of(i * kw, kw), kw)
            gmix[:, at] = dot_nt(grads[m], w_o[at, :]).astype(BF16)

        at_slot = pl.ds(pl.multiple_of(m * ns, ns), ns)
        for g in range(groups):
            gc = slice(g * HD, (g + 1) * HD)
            gm = stacked(gmix, None, g)
            p = probs[m, g]
            kg = kpad[m, :, gc]
            gp = dot_nt(gm, vpad[m, :, gc])
            gv = dot_tn(p.astype(BF16), gm).astype(BF16)
            gs = p * (gp - jnp.sum(p * gp, axis=-1, keepdims=True))
            gs = (gs * scale).astype(BF16)
            gq = dot(gs, kg).astype(BF16)
            gk = dot_tn(gs, stacked(q, m, g)).astype(BF16)
            for h in range(per):
                low = (g * per + h) * HD
                dqkv[:, low : low + HD] = gq[h * count : (h + 1) * count]
            dqkv[:, qw + g * HD : qw + (g + 1) * HD] = gk[:count]
            dqkv[:, qw + kw + g * HD : qw + kw + (g + 1) * HD] = gv[:count]
            ks_all[dp, 0, at_slot, gc] = gk[count : count + ns]
            ks_all[dp, 1, at_slot, gc] = gv[count : count + ns]

        @pl.when(sec > 0)
        def _():
            inv = inv_all[m, :, 0:1]
            weight = (
                jnp.sum(dqkv[:, :qw].astype(F32) * q[m].astype(F32), axis=-1, keepdims=True)
                + jnp.sum(
                    dqkv[:, qw : qw + kw].astype(F32) * kpad[m, 0:count, :].astype(F32),
                    axis=-1,
                    keepdims=True,
                )
                + jnp.sum(
                    dqkv[:, qw + kw :].astype(F32) * vpad[m, 0:count, :].astype(F32),
                    axis=-1,
                    keepdims=True,
                )
            )
            weight = weight * inv * (1.0 / width)

            @pl.loop(0, CHUNKS)
            def _(c):
                term = dot_nt(dqkv[...], w_all[cols(c), :]) * gain[:, cols(c)]
                term = inv * (term - rows[m, :, cols(c)].astype(F32) * weight)
                term = term + jnp.where(mine, grads[m, :, cols(c)].astype(F32), 0.0)
                part_b[m, :, cols(c)] = term.astype(BF16)
                rs_send(part_b, rs_b, rsb_s, rsb_r, m, c)

    low_half = sec < half
    f_at = jnp.where(low_half, 0, nb)
    rf_at = jnp.where(low_half, nb, 0)
    rb_at = jnp.where(low_half, 2 * nb, 3 * nb)
    b_at = jnp.where(low_half, 3 * nb, jnp.where(sec == last, nb, 2 * nb))

    @pl.loop(0, 4 * nb)
    def _(t):
        @pl.when((mate < last) & (t >= rf_at) & (t < rf_at + nb))
        def _():
            reduce(own_f, part_f, rs_f, rows, rsf_s, rsf_r, agf_s, agf_r, t - rf_at, mate + 1)

        @pl.when((t >= f_at) & (t < f_at + nb))
        def _():
            forward(t - f_at)

        @pl.when((t >= b_at) & (t < b_at + nb))
        def _():
            backward(t - b_at)

        @pl.when((mate > 0) & (t >= rb_at) & (t < rb_at + nb))
        def _():
            reduce(own_b, part_b, rs_b, grads, rsb_s, rsb_r, agb_s, agb_r, t - rb_at, mate - 1)

    dp_send(ks_all, ks_s, ks_r)
    me = dp * nmp + mp
    lg_all[me, 0] = dot_nt(ks_all[dp, 0], key_b[0])
    lg_all[me, 1] = dot_nt(ks_all[dp, 1], value_b[0])

    def lg_copy(a, b, source):
        return pltpu.make_async_remote_copy(
            src_ref=lg_all.at[source],
            dst_ref=lg_all.at[source],
            send_sem=lg_s.at[a * nmp + b],
            recv_sem=lg_r.at[a * nmp + b],
            device_id={"dp": lax.rem(dp + a, ndp), "mp": lax.rem(mp + b, nmp)},
            device_id_type=MESH,
        )

    others = [(a, b) for a in range(ndp) for b in range(nmp) if a or b]
    for a, b in others:
        lg_copy(a, b, me).start()
    dp_wait(sn_all, sn_s, sn_r)
    dp_wait(low_all, lo_s, lo_r)
    sn_out[...] = sn_all[...]
    low_out[...] = low_all[...]
    dp_wait(ks_all, ks_s, ks_r)
    ks_out[...] = ks_all[...]
    for a, b in others:
        source = lax.rem(dp - a + ndp, ndp) * nmp + lax.rem(mp - b + nmp, nmp)
        lg_copy(a, b, source).wait_recv()
    for a in range(ndp):
        total = lg_all[a * nmp]
        for b in range(1, nmp):
            total = total + lg_all[a * nmp + b]
        low_total_out[a] = total
    for a, b in others:
        lg_copy(a, b, me).wait_send()

    def settle(copy, active):
        @pl.when(active)
        def _():
            @pl.loop(0, nb * CHUNKS)
            def _(i):
                for d in range(nmp):
                    copy(i // CHUNKS, lax.rem(i, CHUNKS), peer(d)).wait_send()

    settle(lambda m, c, j: rs_copy(part_f, rs_f, rsf_s, rsf_r, m, c, j, mp), sec < last)
    settle(lambda m, c, j: rs_copy(part_b, rs_b, rsb_s, rsb_r, m, c, j, mp), sec > 0)
    settle(lambda m, c, j: ag_copy(own_f, rows, agf_s, agf_r, m, c, j, mp, mate), mate < last)
    settle(lambda m, c, j: ag_copy(own_b, grads, agb_s, agb_r, m, c, j, mp, mate), mate > 0)


def local(ndp, nsec, nmp, hidden_in, slot_hidden, norm_gain, w_query, w_key, w_value, w_out,
          key_a, key_b, value_a, value_b, cotangent):
    nb, count, width = hidden_in.shape
    ns = slot_hidden.shape[2]
    qw, kw = w_query.shape[2], w_key.shape[2]
    rank = key_a.shape[2]
    share = count // nmp
    groups = kw // HD
    per = qw // kw
    padded = -(-(count + ns) // 256) * 256
    total_slots = nb * ns
    slots = slot_hidden.reshape(1, total_slots, width)
    vmem = pl.BlockSpec(memory_space=pltpu.VMEM)
    hbm = pl.BlockSpec(memory_space=pl.ANY)
    dma = pltpu.SemaphoreType.DMA
    many = dma((nb * CHUNKS * nmp,))
    few = dma((max(ndp - 1, 1),))
    sn_shape = (ndp, total_slots, width)
    low_shape = (ndp, 2, total_slots, rank)
    ks_shape = (ndp, 2, total_slots, kw)
    sn_all, low_all, low_total, ks_all = pl.pallas_call(
        functools.partial(kernel, ndp, nsec, nmp),
        out_shape=(
            jax.ShapeDtypeStruct(sn_shape, BF16),
            jax.ShapeDtypeStruct(low_shape, BF16),
            jax.ShapeDtypeStruct(low_shape, F32),
            jax.ShapeDtypeStruct(ks_shape, BF16),
        ),
        in_specs=[hbm, vmem, vmem, hbm, hbm, hbm, hbm, vmem, vmem, vmem, vmem, hbm],
        out_specs=(vmem, vmem, vmem, vmem),
        scratch_shapes=[
            pltpu.VMEM((width, qw + 2 * kw), BF16),
            pltpu.VMEM((qw, width), BF16),
            pltpu.VMEM((nb, count, width), BF16),
            pltpu.VMEM((nb, count, width), BF16),
            pltpu.VMEM((count, width), BF16),
            pltpu.VMEM((nb, count, width), BF16),
            pltpu.VMEM((nb, count, width), BF16),
            pltpu.VMEM((nb, nmp, share, width), BF16),
            pltpu.VMEM((nb, nmp, share, width), BF16),
            pltpu.VMEM((nb, share, width), BF16),
            pltpu.VMEM((nb, share, width), BF16),
            pltpu.VMEM((nb, count, qw), BF16),
            pltpu.VMEM((nb, padded, kw), BF16),
            pltpu.VMEM((nb, padded, kw), BF16),
            pltpu.VMEM((nb, groups, per * count, padded), F32),
            pltpu.VMEM((nb, count, HD), F32),
            pltpu.VMEM((count, qw), BF16),
            pltpu.VMEM((count, qw), BF16),
            pltpu.VMEM((count, qw + 2 * kw), BF16),
            pltpu.VMEM(sn_shape, BF16),
            pltpu.VMEM(low_shape, BF16),
            pltpu.VMEM((ndp * nmp, 2, total_slots, rank), F32),
            pltpu.VMEM(ks_shape, BF16),
            dma((4,)),
            dma((2,)),
            many, many, many, many, many, many, many, many,
            few, few, few, few,
            dma((ndp * nmp,)), dma((ndp * nmp,)),
            few, few,
        ],
        compiler_params=pltpu.CompilerParams(
            collective_id=0, has_side_effects=True, vmem_limit_bytes=58 * 1024 * 1024
        ),
    )(hidden_in, slots, norm_gain, w_query, w_key, w_value, w_out, jnp.swapaxes(key_a, 1, 2), key_b,
      jnp.swapaxes(value_a, 1, 2), value_b, cotangent)
    grad_a = jnp.einsum("psd,ptsr->tdr", sn_all.astype(F32), low_total, precision=HIGH)
    grad_b = jnp.einsum("ptsr,ptsc->trc", low_all, ks_all, preferred_element_type=F32)
    return (grad_a[None], grad_b[None])


def solution(mesh):
    placed = (
        P("dp", None, None),
        P("section", "dp", None, None),
        P("section", None),
        P("section", None, "mp"),
        P("section", None, "mp"),
        P("section", None, "mp"),
        P("section", "mp", None),
        P("section", None, None),
        P("section", None, "mp"),
        P("section", None, None),
        P("section", None, "mp"),
        P("dp", None, None),
    )
    return jax.shard_map(
        functools.partial(local, mesh.shape["dp"], mesh.shape["section"], mesh.shape["mp"]),
        mesh=mesh,
        in_specs=placed,
        out_specs=(P("section", None, None, None), P("section", None, None, "mp")),
        check_vma=False,
    )
```

```python
import functools
import math

import jax
import jax.numpy as jnp
from jax import lax
from jax.experimental import pallas as pl
from jax.experimental.pallas import tpu as pltpu
from jax.sharding import PartitionSpec as P

HD = 128
EPS = 1e-05
NEG = -1e30
HIGH = lax.Precision.HIGHEST
MESH = pl.DeviceIdType.MESH
CHUNKS = 8
SPLIT = 2
F32 = jnp.float32
BF16 = jnp.bfloat16


def dot(a, b):
    return jnp.dot(a, b, preferred_element_type=F32)


def dot_nt(a, b):
    return lax.dot_general(a, b, (((1,), (1,)), ((), ())), preferred_element_type=F32)


def dot_tn(a, b):
    return lax.dot_general(a, b, (((0,), (0,)), ((), ())), preferred_element_type=F32)


def kernel(
    ndp,
    nsec,
    nmp,
    hidden,
    slots,
    gain,
    w_q,
    w_k,
    w_v,
    w_out,
    key_a,
    key_b,
    value_a,
    value_b,
    cot,
    sn_out,
    low_out,
    low_total_out,
    ks_out,
    w_all,
    w_o,
    rows,
    grads,
    xn,
    part_f,
    part_b,
    rs_f,
    rs_b,
    own_f,
    own_b,
    q,
    kpad,
    vpad,
    probs,
    inv_all,
    mixed,
    gmix,
    dqkv,
    sn_all,
    low_all,
    lg_all,
    ks_all,
    w_sem,
    in_sem,
    rsf_s,
    rsf_r,
    rsb_s,
    rsb_r,
    agf_s,
    agf_r,
    agb_s,
    agb_r,
    sn_s,
    sn_r,
    lo_s,
    lo_r,
    lg_s,
    lg_r,
    ks_s,
    ks_r,
):
    dp = lax.axis_index("dp")
    sec = lax.axis_index("section")
    mp = lax.axis_index("mp")
    last = nsec - 1
    half = nsec // 2
    mate = lax.rem(sec + half, nsec)
    nb, count, width = rows.shape
    ns = slots.shape[1] // nb
    share = count // nmp
    ch = width // CHUNKS
    qw = q.shape[2]
    kw = kpad.shape[2]
    groups = kw // HD
    per = qw // kw
    padded = kpad.shape[1]
    scale = 1.0 / math.sqrt(HD)

    loads = [
        pltpu.make_async_copy(w_k.at[0], w_all.at[:, pl.ds(qw, kw)], w_sem.at[0]),
        pltpu.make_async_copy(w_v.at[0], w_all.at[:, pl.ds(qw + kw, kw)], w_sem.at[1]),
        pltpu.make_async_copy(w_q.at[0], w_all.at[:, pl.ds(0, qw)], w_sem.at[2]),
        pltpu.make_async_copy(w_out.at[0], w_o, w_sem.at[3]),
    ]
    for load in loads:
        load.start()
    load_rows = pltpu.make_async_copy(hidden, rows, in_sem.at[0])
    load_cot = pltpu.make_async_copy(cot, grads, in_sem.at[1])

    @pl.when(sec == 0)
    def _():
        load_rows.start()

    @pl.when(sec == last)
    def _():
        load_cot.start()

    bar = pltpu.get_barrier_semaphore()
    for a in range(nsec):
        for b in range(nmp):
            if a or b:
                pl.semaphore_signal(
                    bar,
                    inc=1,
                    device_id={"section": lax.rem(sec + a, nsec), "mp": lax.rem(mp + b, nmp)},
                    device_id_type=MESH,
                )
    for a in range(1, ndp):
        for b in range(nmp):
            pl.semaphore_signal(
                bar,
                inc=1,
                device_id={"dp": lax.rem(dp + a, ndp), "mp": lax.rem(mp + b, nmp)},
                device_id_type=MESH,
            )
    pl.semaphore_wait(bar, nsec * nmp - 1 + (ndp - 1) * nmp)

    def dp_copy(buf, send, recv, a, source):
        return pltpu.make_async_remote_copy(
            src_ref=buf.at[source],
            dst_ref=buf.at[source],
            send_sem=send.at[a - 1],
            recv_sem=recv.at[a - 1],
            device_id={"dp": lax.rem(dp + a, ndp)},
            device_id_type=MESH,
        )

    def dp_send(buf, send, recv):
        for a in range(1, ndp):
            dp_copy(buf, send, recv, a, dp).start()

    def dp_wait(buf, send, recv):
        for a in range(1, ndp):
            dp_copy(buf, send, recv, a, lax.rem(dp - a + ndp, ndp)).wait_recv()
        for a in range(1, ndp):
            dp_copy(buf, send, recv, a, dp).wait_send()

    wide = slots[0].astype(F32)
    inverse = lax.rsqrt(jnp.mean(wide * wide, axis=-1, keepdims=True) + EPS)
    sn_all[dp] = (wide * inverse * gain[...]).astype(BF16)
    dp_send(sn_all, sn_s, sn_r)
    sn = sn_all[dp]
    low_k = dot_nt(sn, key_a[0]).astype(BF16)
    low_v = dot_nt(sn, value_a[0]).astype(BF16)
    low_all[dp, 0] = low_k
    low_all[dp, 1] = low_v
    dp_send(low_all, lo_s, lo_r)
    loads[0].wait()
    slot_k = (dot(sn, w_all[:, qw : qw + kw]) + dot(low_k, key_b[0])).astype(BF16)
    loads[1].wait()
    slot_v = (dot(sn, w_all[:, qw + kw : qw + 2 * kw]) + dot(low_v, value_b[0])).astype(BF16)
    kpad[...] = jnp.zeros_like(kpad)
    vpad[...] = jnp.zeros_like(vpad)
    for m in range(nb):
        kpad[m, count : count + ns, :] = slot_k[m * ns : (m + 1) * ns]
        vpad[m, count : count + ns, :] = slot_v[m * ns : (m + 1) * ns]
    loads[2].wait()
    loads[3].wait()

    @pl.when(sec == 0)
    def _():
        load_rows.wait()

    @pl.when(sec == last)
    def _():
        load_cot.wait()

    mine = lax.broadcasted_iota(jnp.int32, (count, 1), 0) // share == mp

    def cols(c):
        return pl.ds(pl.multiple_of(c * ch, ch), ch)

    def wide_cols(c):
        return pl.ds(pl.multiple_of(c * ch * SPLIT, ch * SPLIT), ch * SPLIT)

    def share_rows(j):
        return pl.ds(pl.multiple_of(j * share, share), share)

    def sem_at(m, c, j):
        return (m * CHUNKS + c) * nmp + j

    def rs_copy(part, land, send, recv, m, c, to, source):
        return pltpu.make_async_remote_copy(
            src_ref=part.at[m, share_rows(to), cols(c)],
            dst_ref=land.at[m, source, :, cols(c)],
            send_sem=send.at[sem_at(m, c, to)],
            recv_sem=recv.at[sem_at(m, c, source)],
            device_id={"section": mate, "mp": to},
            device_id_type=MESH,
        )

    def ag_copy(own, land, send, recv, m, c, to, source, section):
        return pltpu.make_async_remote_copy(
            src_ref=own.at[m, :, cols(c)],
            dst_ref=land.at[m, share_rows(source), cols(c)],
            send_sem=send.at[sem_at(m, c, to)],
            recv_sem=recv.at[sem_at(m, c, source)],
            device_id={"section": section, "mp": to},
            device_id_type=MESH,
        )

    def peer(d):
        return lax.rem(mp + d, nmp)

    def rs_send(part, land, send, recv, m, c):
        for d in range(nmp):
            rs_copy(part, land, send, recv, m, c, peer(d), mp).start()

    def ag_send(own, land, send, recv, m, c, section):
        for d in range(nmp):
            ag_copy(own, land, send, recv, m, c, peer(d), mp, section).start()

    def ag_wait(own, land, send, recv, m, section):
        @pl.loop(0, CHUNKS)
        def _(c):
            for j in range(nmp):
                ag_copy(own, land, send, recv, m, c, j, j, section).wait_recv()

    def reduce(own, part, land, spread, rs_s, rs_r, ag_s, ag_r, m, section):
        @pl.loop(0, CHUNKS)
        def _(c):
            total = None
            for j in range(nmp):
                rs_copy(part, land, rs_s, rs_r, m, c, j, j).wait_recv()
            for j in range(nmp):
                piece = land[m, j, :, cols(c)].astype(F32)
                total = piece if total is None else total + piece
            own[m, :, cols(c)] = total.astype(BF16)
            ag_send(own, spread, ag_s, ag_r, m, c, section)

    def stacked(ref, lead, g):
        parts = []
        for h in range(per):
            low = (g * per + h) * HD
            parts.append(ref[lead, :, low : low + HD])
        return jnp.concatenate(parts, axis=0)

    def forward(m):
        @pl.when(sec > 0)
        def _():
            ag_wait(own_f, rows, agf_s, agf_r, m, mate)

        @pl.loop(0, count // 16)
        def _(i):
            at = pl.ds(pl.multiple_of(i * 16, 16), 16)
            x = rows[m, at, :].astype(F32)
            inv = lax.rsqrt(jnp.mean(x * x, axis=-1, keepdims=True) + EPS)
            xn[at, :] = (x * inv * gain[...]).astype(BF16)
            inv_all[m, at, :] = jnp.broadcast_to(inv, (16, HD))

        qkv = dot(xn[...], w_all[...]).astype(BF16)
        q[m] = qkv[:, :qw]
        kpad[m, 0:count, :] = qkv[:, qw : qw + kw]
        vpad[m, 0:count, :] = qkv[:, qw + kw :]
        i_at = lax.rem(lax.broadcasted_iota(jnp.int32, (per * count, padded), 0), count)
        j_at = lax.broadcasted_iota(jnp.int32, (per * count, padded), 1)
        seen = (j_at <= i_at) | ((j_at >= count) & (j_at < count + ns))
        for g in range(groups):
            gc = slice(g * HD, (g + 1) * HD)
            scores = dot_nt(stacked(q, m, g), kpad[m, :, gc]) * scale
            scores = jnp.where(seen, scores, NEG)
            e = jnp.exp(scores - jnp.max(scores, axis=-1, keepdims=True))
            p = e / jnp.sum(e, axis=-1, keepdims=True)
            probs[m, g] = p
            o = dot(p.astype(BF16), vpad[m, :, gc]).astype(BF16)
            for h in range(per):
                low = (g * per + h) * HD
                mixed[:, low : low + HD] = o[h * count : (h + 1) * count]

        @pl.when(sec < last)
        def _():
            @pl.loop(0, CHUNKS // SPLIT)
            def _(c):
                term = dot(mixed[...], w_o[:, wide_cols(c)])
                term = term + jnp.where(mine, rows[m, :, wide_cols(c)].astype(F32), 0.0)
                part_f[m, :, wide_cols(c)] = term.astype(BF16)
                for k in range(SPLIT):
                    rs_send(part_f, rs_f, rsf_s, rsf_r, m, c * SPLIT + k)

    def mix_back(m):
        gmix[m] = dot_nt(grads[m], w_o[...]).astype(BF16)

    def backward(m):
        @pl.when(sec < last)
        def _():
            ag_wait(own_b, grads, agb_s, agb_r, m, mate)
            mix_back(m)

        at_slot = pl.ds(pl.multiple_of(m * ns, ns), ns)
        for g in range(groups):
            gc = slice(g * HD, (g + 1) * HD)
            gm = stacked(gmix, m, g)
            p = probs[m, g]
            kg = kpad[m, :, gc]
            gp = dot_nt(gm, vpad[m, :, gc])
            gv = dot_tn(p.astype(BF16), gm).astype(BF16)
            gs = p * (gp - jnp.sum(p * gp, axis=-1, keepdims=True))
            gs = (gs * scale).astype(BF16)
            gq = dot(gs, kg).astype(BF16)
            gk = dot_tn(gs, stacked(q, m, g)).astype(BF16)
            for h in range(per):
                low = (g * per + h) * HD
                dqkv[:, low : low + HD] = gq[h * count : (h + 1) * count]
            dqkv[:, qw + g * HD : qw + (g + 1) * HD] = gk[:count]
            dqkv[:, qw + kw + g * HD : qw + kw + (g + 1) * HD] = gv[:count]
            ks_all[dp, 0, at_slot, gc] = gk[count : count + ns]
            ks_all[dp, 1, at_slot, gc] = gv[count : count + ns]

        @pl.when(sec > 0)
        def _():
            inv = inv_all[m, :, 0:1]
            weight = (
                jnp.sum(dqkv[:, :qw].astype(F32) * q[m].astype(F32), axis=-1, keepdims=True)
                + jnp.sum(
                    dqkv[:, qw : qw + kw].astype(F32) * kpad[m, 0:count, :].astype(F32),
                    axis=-1,
                    keepdims=True,
                )
                + jnp.sum(
                    dqkv[:, qw + kw :].astype(F32) * vpad[m, 0:count, :].astype(F32),
                    axis=-1,
                    keepdims=True,
                )
            )
            weight = weight * inv * (1.0 / width)

            @pl.loop(0, CHUNKS // SPLIT)
            def _(c):
                term = dot_nt(dqkv[...], w_all[wide_cols(c), :]) * gain[:, wide_cols(c)]
                term = inv * (term - rows[m, :, wide_cols(c)].astype(F32) * weight)
                term = term + jnp.where(mine, grads[m, :, wide_cols(c)].astype(F32), 0.0)
                part_b[m, :, wide_cols(c)] = term.astype(BF16)
                for k in range(SPLIT):
                    rs_send(part_b, rs_b, rsb_s, rsb_r, m, c * SPLIT + k)

    @pl.when(sec == last)
    def _():
        @pl.loop(0, nb)
        def _(m):
            mix_back(m)

    low_half = sec < half
    f_at = jnp.where(low_half, 0, nb)
    rf_at = jnp.where(low_half, nb, 0)
    rb_at = jnp.where(low_half, 2 * nb, 3 * nb)
    b_at = jnp.where(low_half, 3 * nb, jnp.where(sec == last, nb, 2 * nb))

    @pl.loop(0, 4 * nb)
    def _(t):
        @pl.when((mate < last) & (t >= rf_at) & (t < rf_at + nb))
        def _():
            reduce(own_f, part_f, rs_f, rows, rsf_s, rsf_r, agf_s, agf_r, t - rf_at, mate + 1)

        @pl.when((t >= f_at) & (t < f_at + nb))
        def _():
            forward(t - f_at)

        @pl.when((t >= b_at) & (t < b_at + nb))
        def _():
            backward(t - b_at)

        @pl.when((mate > 0) & (t >= rb_at) & (t < rb_at + nb))
        def _():
            reduce(own_b, part_b, rs_b, grads, rsb_s, rsb_r, agb_s, agb_r, t - rb_at, mate - 1)

    dp_send(ks_all, ks_s, ks_r)
    me = dp * nmp + mp
    lg_all[me, 0] = dot_nt(ks_all[dp, 0], key_b[0])
    lg_all[me, 1] = dot_nt(ks_all[dp, 1], value_b[0])

    def lg_copy(a, b, source):
        return pltpu.make_async_remote_copy(
            src_ref=lg_all.at[source],
            dst_ref=lg_all.at[source],
            send_sem=lg_s.at[a * nmp + b],
            recv_sem=lg_r.at[a * nmp + b],
            device_id={"dp": lax.rem(dp + a, ndp), "mp": lax.rem(mp + b, nmp)},
            device_id_type=MESH,
        )

    others = [(a, b) for a in range(ndp) for b in range(nmp) if a or b]
    for a, b in others:
        lg_copy(a, b, me).start()
    dp_wait(sn_all, sn_s, sn_r)
    dp_wait(low_all, lo_s, lo_r)
    sn_out[...] = sn_all[...]
    low_out[...] = low_all[...]
    dp_wait(ks_all, ks_s, ks_r)
    ks_out[...] = ks_all[...]
    for a, b in others:
        source = lax.rem(dp - a + ndp, ndp) * nmp + lax.rem(mp - b + nmp, nmp)
        lg_copy(a, b, source).wait_recv()
    for a in range(ndp):
        total = lg_all[a * nmp]
        for b in range(1, nmp):
            total = total + lg_all[a * nmp + b]
        low_total_out[a] = total
    for a, b in others:
        lg_copy(a, b, me).wait_send()

    def settle(copy, active):
        @pl.when(active)
        def _():
            @pl.loop(0, nb * CHUNKS)
            def _(i):
                for d in range(nmp):
                    copy(i // CHUNKS, lax.rem(i, CHUNKS), peer(d)).wait_send()

    settle(lambda m, c, j: rs_copy(part_f, rs_f, rsf_s, rsf_r, m, c, j, mp), sec < last)
    settle(lambda m, c, j: rs_copy(part_b, rs_b, rsb_s, rsb_r, m, c, j, mp), sec > 0)
    settle(lambda m, c, j: ag_copy(own_f, rows, agf_s, agf_r, m, c, j, mp, mate), mate < last)
    settle(lambda m, c, j: ag_copy(own_b, grads, agb_s, agb_r, m, c, j, mp, mate), mate > 0)


def local(ndp, nsec, nmp, hidden_in, slot_hidden, norm_gain, w_query, w_key, w_value, w_out,
          key_a, key_b, value_a, value_b, cotangent):
    nb, count, width = hidden_in.shape
    ns = slot_hidden.shape[2]
    qw, kw = w_query.shape[2], w_key.shape[2]
    rank = key_a.shape[2]
    share = count // nmp
    groups = kw // HD
    per = qw // kw
    padded = -(-(count + ns) // 256) * 256
    total_slots = nb * ns
    slots = slot_hidden.reshape(1, total_slots, width)
    vmem = pl.BlockSpec(memory_space=pltpu.VMEM)
    hbm = pl.BlockSpec(memory_space=pl.ANY)
    dma = pltpu.SemaphoreType.DMA
    many = dma((nb * CHUNKS * nmp,))
    few = dma((max(ndp - 1, 1),))
    sn_shape = (ndp, total_slots, width)
    low_shape = (ndp, 2, total_slots, rank)
    ks_shape = (ndp, 2, total_slots, kw)
    sn_all, low_all, low_total, ks_all = pl.pallas_call(
        functools.partial(kernel, ndp, nsec, nmp),
        out_shape=(
            jax.ShapeDtypeStruct(sn_shape, BF16),
            jax.ShapeDtypeStruct(low_shape, BF16),
            jax.ShapeDtypeStruct(low_shape, F32),
            jax.ShapeDtypeStruct(ks_shape, BF16),
        ),
        in_specs=[hbm, vmem, vmem, hbm, hbm, hbm, hbm, vmem, vmem, vmem, vmem, hbm],
        out_specs=(vmem, vmem, vmem, vmem),
        scratch_shapes=[
            pltpu.VMEM((width, qw + 2 * kw), BF16),
            pltpu.VMEM((qw, width), BF16),
            pltpu.VMEM((nb, count, width), BF16),
            pltpu.VMEM((nb, count, width), BF16),
            pltpu.VMEM((count, width), BF16),
            pltpu.VMEM((nb, count, width), BF16),
            pltpu.VMEM((nb, count, width), BF16),
            pltpu.VMEM((nb, nmp, share, width), BF16),
            pltpu.VMEM((nb, nmp, share, width), BF16),
            pltpu.VMEM((nb, share, width), BF16),
            pltpu.VMEM((nb, share, width), BF16),
            pltpu.VMEM((nb, count, qw), BF16),
            pltpu.VMEM((nb, padded, kw), BF16),
            pltpu.VMEM((nb, padded, kw), BF16),
            pltpu.VMEM((nb, groups, per * count, padded), F32),
            pltpu.VMEM((nb, count, HD), F32),
            pltpu.VMEM((count, qw), BF16),
            pltpu.VMEM((nb, count, qw), BF16),
            pltpu.VMEM((count, qw + 2 * kw), BF16),
            pltpu.VMEM(sn_shape, BF16),
            pltpu.VMEM(low_shape, BF16),
            pltpu.VMEM((ndp * nmp, 2, total_slots, rank), F32),
            pltpu.VMEM(ks_shape, BF16),
            dma((4,)),
            dma((2,)),
            many, many, many, many, many, many, many, many,
            few, few, few, few,
            dma((ndp * nmp,)), dma((ndp * nmp,)),
            few, few,
        ],
        compiler_params=pltpu.CompilerParams(
            collective_id=0, has_side_effects=True, vmem_limit_bytes=58 * 1024 * 1024
        ),
    )(hidden_in, slots, norm_gain, w_query, w_key, w_value, w_out, jnp.swapaxes(key_a, 1, 2), key_b,
      jnp.swapaxes(value_a, 1, 2), value_b, cotangent)
    grad_a = jnp.einsum("psd,ptsr->tdr", sn_all.astype(F32), low_total, precision=HIGH)
    grad_b = jnp.einsum("ptsr,ptsc->trc", low_all, ks_all, preferred_element_type=F32)
    return (grad_a[None], grad_b[None])


def solution(mesh):
    placed = (
        P("dp", None, None),
        P("section", "dp", None, None),
        P("section", None),
        P("section", None, "mp"),
        P("section", None, "mp"),
        P("section", None, "mp"),
        P("section", "mp", None),
        P("section", None, None),
        P("section", None, "mp"),
        P("section", None, None),
        P("section", None, "mp"),
        P("dp", None, None),
    )
    return jax.shard_map(
        functools.partial(local, mesh.shape["dp"], mesh.shape["section"], mesh.shape["mp"]),
        mesh=mesh,
        in_specs=placed,
        out_specs=(P("section", None, None, None), P("section", None, None, "mp")),
        check_vma=False,
    )
```

```python
import functools
import math

import jax
import jax.numpy as jnp
from jax import lax
from jax.experimental import pallas as pl
from jax.experimental.pallas import tpu as pltpu
from jax.sharding import PartitionSpec as P

HD = 128
EPS = 1e-05
NEG = -1e30
HIGH = lax.Precision.HIGHEST
MESH = pl.DeviceIdType.MESH
CHUNKS = 8
SPLIT = 2
F32 = jnp.float32
BF16 = jnp.bfloat16


def dot(a, b):
    return jnp.dot(a, b, preferred_element_type=F32)


def dot_nt(a, b):
    return lax.dot_general(a, b, (((1,), (1,)), ((), ())), preferred_element_type=F32)


def dot_tn(a, b):
    return lax.dot_general(a, b, (((0,), (0,)), ((), ())), preferred_element_type=F32)


def kernel(
    ndp,
    nsec,
    nmp,
    hidden,
    slots,
    gain,
    w_q,
    w_k,
    w_v,
    w_out,
    key_a,
    key_b,
    value_a,
    value_b,
    cot,
    sn_out,
    low_out,
    low_total_out,
    ks_out,
    w_all,
    w_o,
    rows,
    grads,
    xn,
    part_f,
    part_b,
    rs_f,
    rs_b,
    own_f,
    own_b,
    q,
    kpad,
    vpad,
    probs,
    inv_all,
    mixed,
    gmix,
    dqkv,
    sn_all,
    low_all,
    lg_all,
    ks_all,
    w_sem,
    in_sem,
    rsf_s,
    rsf_r,
    rsb_s,
    rsb_r,
    agf_s,
    agf_r,
    agb_s,
    agb_r,
    sn_s,
    sn_r,
    lo_s,
    lo_r,
    lg_s,
    lg_r,
    ks_s,
    ks_r,
):
    dp = lax.axis_index("dp")
    sec = lax.axis_index("section")
    mp = lax.axis_index("mp")
    last = nsec - 1
    half = nsec // 2
    f_from = lax.rem(sec + 1, last)
    f_owner = lax.rem(sec + last - 1, last)
    b_from = last - lax.rem(last - sec + 1, last)
    b_owner = last - lax.rem(last - sec + last - 1, last)
    nb, count, width = rows.shape
    ns = slots.shape[1] // nb
    share = count // nmp
    ch = width // CHUNKS
    qw = q.shape[2]
    kw = kpad.shape[2]
    groups = kw // HD
    per = qw // kw
    padded = kpad.shape[1]
    scale = 1.0 / math.sqrt(HD)

    loads = [
        pltpu.make_async_copy(w_k.at[0], w_all.at[:, pl.ds(qw, kw)], w_sem.at[0]),
        pltpu.make_async_copy(w_v.at[0], w_all.at[:, pl.ds(qw + kw, kw)], w_sem.at[1]),
        pltpu.make_async_copy(w_q.at[0], w_all.at[:, pl.ds(0, qw)], w_sem.at[2]),
        pltpu.make_async_copy(w_out.at[0], w_o, w_sem.at[3]),
    ]
    for load in loads:
        load.start()
    load_rows = pltpu.make_async_copy(hidden, rows, in_sem.at[0])
    load_cot = pltpu.make_async_copy(cot, grads, in_sem.at[1])

    @pl.when(sec == 0)
    def _():
        load_rows.start()

    @pl.when(sec == last)
    def _():
        load_cot.start()

    bar = pltpu.get_barrier_semaphore()
    for a in range(nsec):
        for b in range(nmp):
            if a or b:
                pl.semaphore_signal(
                    bar,
                    inc=1,
                    device_id={"section": lax.rem(sec + a, nsec), "mp": lax.rem(mp + b, nmp)},
                    device_id_type=MESH,
                )
    for a in range(1, ndp):
        for b in range(nmp):
            pl.semaphore_signal(
                bar,
                inc=1,
                device_id={"dp": lax.rem(dp + a, ndp), "mp": lax.rem(mp + b, nmp)},
                device_id_type=MESH,
            )
    pl.semaphore_wait(bar, nsec * nmp - 1 + (ndp - 1) * nmp)

    def dp_copy(buf, send, recv, a, source):
        return pltpu.make_async_remote_copy(
            src_ref=buf.at[source],
            dst_ref=buf.at[source],
            send_sem=send.at[a - 1],
            recv_sem=recv.at[a - 1],
            device_id={"dp": lax.rem(dp + a, ndp)},
            device_id_type=MESH,
        )

    def dp_send(buf, send, recv):
        for a in range(1, ndp):
            dp_copy(buf, send, recv, a, dp).start()

    def dp_wait(buf, send, recv):
        for a in range(1, ndp):
            dp_copy(buf, send, recv, a, lax.rem(dp - a + ndp, ndp)).wait_recv()
        for a in range(1, ndp):
            dp_copy(buf, send, recv, a, dp).wait_send()

    wide = slots[0].astype(F32)
    inverse = lax.rsqrt(jnp.mean(wide * wide, axis=-1, keepdims=True) + EPS)
    sn_all[dp] = (wide * inverse * gain[...]).astype(BF16)
    dp_send(sn_all, sn_s, sn_r)
    sn = sn_all[dp]
    low_k = dot_nt(sn, key_a[0]).astype(BF16)
    low_v = dot_nt(sn, value_a[0]).astype(BF16)
    low_all[dp, 0] = low_k
    low_all[dp, 1] = low_v
    dp_send(low_all, lo_s, lo_r)
    loads[0].wait()
    slot_k = (dot(sn, w_all[:, qw : qw + kw]) + dot(low_k, key_b[0])).astype(BF16)
    loads[1].wait()
    slot_v = (dot(sn, w_all[:, qw + kw : qw + 2 * kw]) + dot(low_v, value_b[0])).astype(BF16)
    kpad[...] = jnp.zeros_like(kpad)
    vpad[...] = jnp.zeros_like(vpad)
    for m in range(nb):
        kpad[m, count : count + ns, :] = slot_k[m * ns : (m + 1) * ns]
        vpad[m, count : count + ns, :] = slot_v[m * ns : (m + 1) * ns]
    loads[2].wait()
    loads[3].wait()

    @pl.when(sec == 0)
    def _():
        load_rows.wait()

    @pl.when(sec == last)
    def _():
        load_cot.wait()

    mine = lax.broadcasted_iota(jnp.int32, (count, 1), 0) // share == mp

    def cols(c):
        return pl.ds(pl.multiple_of(c * ch, ch), ch)

    def wide_cols(c):
        return pl.ds(pl.multiple_of(c * ch * SPLIT, ch * SPLIT), ch * SPLIT)

    def share_rows(j):
        return pl.ds(pl.multiple_of(j * share, share), share)

    def sem_at(m, c, j):
        return (m * CHUNKS + c) * nmp + j

    def rs_copy(part, land, send, recv, m, c, to, source):
        return pltpu.make_async_remote_copy(
            src_ref=part.at[m, share_rows(to), cols(c)],
            dst_ref=land.at[m, source, :, cols(c)],
            send_sem=send.at[sem_at(m, c, to)],
            recv_sem=recv.at[sem_at(m, c, source)],
            device_id={"section": f_owner if part is part_f else b_owner, "mp": to},
            device_id_type=MESH,
        )

    def ag_copy(own, land, send, recv, m, c, to, source, section):
        return pltpu.make_async_remote_copy(
            src_ref=own.at[m, :, cols(c)],
            dst_ref=land.at[m, share_rows(source), cols(c)],
            send_sem=send.at[sem_at(m, c, to)],
            recv_sem=recv.at[sem_at(m, c, source)],
            device_id={"section": section, "mp": to},
            device_id_type=MESH,
        )

    def peer(d):
        return lax.rem(mp + d, nmp)

    def rs_send(part, land, send, recv, m, c):
        for d in range(nmp):
            rs_copy(part, land, send, recv, m, c, peer(d), mp).start()

    def ag_send(own, land, send, recv, m, c, section):
        for d in range(nmp):
            ag_copy(own, land, send, recv, m, c, peer(d), mp, section).start()

    def ag_wait(own, land, send, recv, m, section):
        @pl.loop(0, CHUNKS)
        def _(c):
            for j in range(nmp):
                ag_copy(own, land, send, recv, m, c, j, j, section).wait_recv()

    def reduce(own, part, land, spread, rs_s, rs_r, ag_s, ag_r, m, section):
        @pl.loop(0, CHUNKS)
        def _(c):
            total = None
            for j in range(nmp):
                rs_copy(part, land, rs_s, rs_r, m, c, j, j).wait_recv()
            for j in range(nmp):
                piece = land[m, j, :, cols(c)].astype(F32)
                total = piece if total is None else total + piece
            own[m, :, cols(c)] = total.astype(BF16)
            ag_send(own, spread, ag_s, ag_r, m, c, section)

    def stacked(ref, lead, g):
        parts = []
        for h in range(per):
            low = (g * per + h) * HD
            parts.append(ref[lead, :, low : low + HD])
        return jnp.concatenate(parts, axis=0)

    def forward(m):
        @pl.when(sec > 0)
        def _():
            ag_wait(own_f, rows, agf_s, agf_r, m, lax.rem(sec + 1, nsec))

        @pl.loop(0, count // 16)
        def _(i):
            at = pl.ds(pl.multiple_of(i * 16, 16), 16)
            x = rows[m, at, :].astype(F32)
            inv = lax.rsqrt(jnp.mean(x * x, axis=-1, keepdims=True) + EPS)
            xn[at, :] = (x * inv * gain[...]).astype(BF16)
            inv_all[m, at, :] = jnp.broadcast_to(inv, (16, HD))

        qkv = dot(xn[...], w_all[...]).astype(BF16)
        q[m] = qkv[:, :qw]
        kpad[m, 0:count, :] = qkv[:, qw : qw + kw]
        vpad[m, 0:count, :] = qkv[:, qw + kw :]
        i_at = lax.rem(lax.broadcasted_iota(jnp.int32, (per * count, padded), 0), count)
        j_at = lax.broadcasted_iota(jnp.int32, (per * count, padded), 1)
        seen = (j_at <= i_at) | ((j_at >= count) & (j_at < count + ns))
        for g in range(groups):
            gc = slice(g * HD, (g + 1) * HD)
            scores = dot_nt(stacked(q, m, g), kpad[m, :, gc]) * scale
            scores = jnp.where(seen, scores, NEG)
            e = jnp.exp(scores - jnp.max(scores, axis=-1, keepdims=True))
            p = e / jnp.sum(e, axis=-1, keepdims=True)
            probs[m, g] = p
            o = dot(p.astype(BF16), vpad[m, :, gc]).astype(BF16)
            for h in range(per):
                low = (g * per + h) * HD
                mixed[:, low : low + HD] = o[h * count : (h + 1) * count]

        @pl.when(sec < last)
        def _():
            @pl.loop(0, CHUNKS // SPLIT)
            def _(c):
                term = dot(mixed[...], w_o[:, wide_cols(c)])
                term = term + jnp.where(mine, rows[m, :, wide_cols(c)].astype(F32), 0.0)
                part_f[m, :, wide_cols(c)] = term.astype(BF16)
                for k in range(SPLIT):
                    rs_send(part_f, rs_f, rsf_s, rsf_r, m, c * SPLIT + k)

    def mix_back(m):
        gmix[m] = dot_nt(grads[m], w_o[...]).astype(BF16)

    def backward(m):
        @pl.when(sec < last)
        def _():
            ag_wait(own_b, grads, agb_s, agb_r, m, lax.rem(sec + 1, nsec))
            mix_back(m)

        at_slot = pl.ds(pl.multiple_of(m * ns, ns), ns)
        for g in range(groups):
            gc = slice(g * HD, (g + 1) * HD)
            gm = stacked(gmix, m, g)
            p = probs[m, g]
            kg = kpad[m, :, gc]
            gp = dot_nt(gm, vpad[m, :, gc])
            gv = dot_tn(p.astype(BF16), gm).astype(BF16)
            gs = p * (gp - jnp.sum(p * gp, axis=-1, keepdims=True))
            gs = (gs * scale).astype(BF16)
            gq = dot(gs, kg).astype(BF16)
            gk = dot_tn(gs, stacked(q, m, g)).astype(BF16)
            for h in range(per):
                low = (g * per + h) * HD
                dqkv[:, low : low + HD] = gq[h * count : (h + 1) * count]
            dqkv[:, qw + g * HD : qw + (g + 1) * HD] = gk[:count]
            dqkv[:, qw + kw + g * HD : qw + kw + (g + 1) * HD] = gv[:count]
            ks_all[dp, 0, at_slot, gc] = gk[count : count + ns]
            ks_all[dp, 1, at_slot, gc] = gv[count : count + ns]

        @pl.when(sec > 0)
        def _():
            inv = inv_all[m, :, 0:1]
            weight = (
                jnp.sum(dqkv[:, :qw].astype(F32) * q[m].astype(F32), axis=-1, keepdims=True)
                + jnp.sum(
                    dqkv[:, qw : qw + kw].astype(F32) * kpad[m, 0:count, :].astype(F32),
                    axis=-1,
                    keepdims=True,
                )
                + jnp.sum(
                    dqkv[:, qw + kw :].astype(F32) * vpad[m, 0:count, :].astype(F32),
                    axis=-1,
                    keepdims=True,
                )
            )
            weight = weight * inv * (1.0 / width)

            @pl.loop(0, CHUNKS // SPLIT)
            def _(c):
                term = dot_nt(dqkv[...], w_all[wide_cols(c), :]) * gain[:, wide_cols(c)]
                term = inv * (term - rows[m, :, wide_cols(c)].astype(F32) * weight)
                term = term + jnp.where(mine, grads[m, :, wide_cols(c)].astype(F32), 0.0)
                part_b[m, :, wide_cols(c)] = term.astype(BF16)
                for k in range(SPLIT):
                    rs_send(part_b, rs_b, rsb_s, rsb_r, m, c * SPLIT + k)

    @pl.when(sec == last)
    def _():
        @pl.loop(0, nb)
        def _(m):
            mix_back(m)

    low_half = sec < half
    f_at = jnp.where(low_half, 0, nb)
    rf_at = jnp.where(low_half, nb, 0)
    rb_at = jnp.where(low_half, 2 * nb, 3 * nb)
    b_at = jnp.where(low_half, 3 * nb, jnp.where(sec == last, nb, 2 * nb))

    @pl.loop(0, 4 * nb)
    def _(t):
        @pl.when((sec < last) & (t >= rf_at) & (t < rf_at + nb))
        def _():
            reduce(own_f, part_f, rs_f, rows, rsf_s, rsf_r, agf_s, agf_r, t - rf_at, f_from + 1)

        @pl.when((t >= f_at) & (t < f_at + nb))
        def _():
            forward(t - f_at)

        @pl.when((t >= b_at) & (t < b_at + nb))
        def _():
            backward(t - b_at)

        @pl.when((sec > 0) & (t >= rb_at) & (t < rb_at + nb))
        def _():
            reduce(own_b, part_b, rs_b, grads, rsb_s, rsb_r, agb_s, agb_r, t - rb_at, b_from - 1)

    dp_send(ks_all, ks_s, ks_r)
    me = dp * nmp + mp
    lg_all[me, 0] = dot_nt(ks_all[dp, 0], key_b[0])
    lg_all[me, 1] = dot_nt(ks_all[dp, 1], value_b[0])

    def lg_copy(a, b, source):
        return pltpu.make_async_remote_copy(
            src_ref=lg_all.at[source],
            dst_ref=lg_all.at[source],
            send_sem=lg_s.at[a * nmp + b],
            recv_sem=lg_r.at[a * nmp + b],
            device_id={"dp": lax.rem(dp + a, ndp), "mp": lax.rem(mp + b, nmp)},
            device_id_type=MESH,
        )

    others = [(a, b) for a in range(ndp) for b in range(nmp) if a or b]
    for a, b in others:
        lg_copy(a, b, me).start()
    dp_wait(sn_all, sn_s, sn_r)
    dp_wait(low_all, lo_s, lo_r)
    sn_out[...] = sn_all[...]
    low_out[...] = low_all[...]
    dp_wait(ks_all, ks_s, ks_r)
    ks_out[...] = ks_all[...]
    for a, b in others:
        source = lax.rem(dp - a + ndp, ndp) * nmp + lax.rem(mp - b + nmp, nmp)
        lg_copy(a, b, source).wait_recv()
    for a in range(ndp):
        total = lg_all[a * nmp]
        for b in range(1, nmp):
            total = total + lg_all[a * nmp + b]
        low_total_out[a] = total
    for a, b in others:
        lg_copy(a, b, me).wait_send()

    def settle(copy, active):
        @pl.when(active)
        def _():
            @pl.loop(0, nb * CHUNKS)
            def _(i):
                for d in range(nmp):
                    copy(i // CHUNKS, lax.rem(i, CHUNKS), peer(d)).wait_send()

    settle(lambda m, c, j: rs_copy(part_f, rs_f, rsf_s, rsf_r, m, c, j, mp), sec < last)
    settle(lambda m, c, j: rs_copy(part_b, rs_b, rsb_s, rsb_r, m, c, j, mp), sec > 0)
    settle(lambda m, c, j: ag_copy(own_f, rows, agf_s, agf_r, m, c, j, mp, f_from + 1), sec < last)
    settle(lambda m, c, j: ag_copy(own_b, grads, agb_s, agb_r, m, c, j, mp, b_from - 1), sec > 0)


def local(ndp, nsec, nmp, hidden_in, slot_hidden, norm_gain, w_query, w_key, w_value, w_out,
          key_a, key_b, value_a, value_b, cotangent):
    nb, count, width = hidden_in.shape
    ns = slot_hidden.shape[2]
    qw, kw = w_query.shape[2], w_key.shape[2]
    rank = key_a.shape[2]
    share = count // nmp
    groups = kw // HD
    per = qw // kw
    padded = -(-(count + ns) // 256) * 256
    total_slots = nb * ns
    slots = slot_hidden.reshape(1, total_slots, width)
    vmem = pl.BlockSpec(memory_space=pltpu.VMEM)
    hbm = pl.BlockSpec(memory_space=pl.ANY)
    dma = pltpu.SemaphoreType.DMA
    many = dma((nb * CHUNKS * nmp,))
    few = dma((max(ndp - 1, 1),))
    sn_shape = (ndp, total_slots, width)
    low_shape = (ndp, 2, total_slots, rank)
    ks_shape = (ndp, 2, total_slots, kw)
    sn_all, low_all, low_total, ks_all = pl.pallas_call(
        functools.partial(kernel, ndp, nsec, nmp),
        out_shape=(
            jax.ShapeDtypeStruct(sn_shape, BF16),
            jax.ShapeDtypeStruct(low_shape, BF16),
            jax.ShapeDtypeStruct(low_shape, F32),
            jax.ShapeDtypeStruct(ks_shape, BF16),
        ),
        in_specs=[hbm, vmem, vmem, hbm, hbm, hbm, hbm, vmem, vmem, vmem, vmem, hbm],
        out_specs=(vmem, vmem, vmem, vmem),
        scratch_shapes=[
            pltpu.VMEM((width, qw + 2 * kw), BF16),
            pltpu.VMEM((qw, width), BF16),
            pltpu.VMEM((nb, count, width), BF16),
            pltpu.VMEM((nb, count, width), BF16),
            pltpu.VMEM((count, width), BF16),
            pltpu.VMEM((nb, count, width), BF16),
            pltpu.VMEM((nb, count, width), BF16),
            pltpu.VMEM((nb, nmp, share, width), BF16),
            pltpu.VMEM((nb, nmp, share, width), BF16),
            pltpu.VMEM((nb, share, width), BF16),
            pltpu.VMEM((nb, share, width), BF16),
            pltpu.VMEM((nb, count, qw), BF16),
            pltpu.VMEM((nb, padded, kw), BF16),
            pltpu.VMEM((nb, padded, kw), BF16),
            pltpu.VMEM((nb, groups, per * count, padded), F32),
            pltpu.VMEM((nb, count, HD), F32),
            pltpu.VMEM((count, qw), BF16),
            pltpu.VMEM((nb, count, qw), BF16),
            pltpu.VMEM((count, qw + 2 * kw), BF16),
            pltpu.VMEM(sn_shape, BF16),
            pltpu.VMEM(low_shape, BF16),
            pltpu.VMEM((ndp * nmp, 2, total_slots, rank), F32),
            pltpu.VMEM(ks_shape, BF16),
            dma((4,)),
            dma((2,)),
            many, many, many, many, many, many, many, many,
            few, few, few, few,
            dma((ndp * nmp,)), dma((ndp * nmp,)),
            few, few,
        ],
        compiler_params=pltpu.CompilerParams(
            collective_id=0, has_side_effects=True, vmem_limit_bytes=58 * 1024 * 1024
        ),
    )(hidden_in, slots, norm_gain, w_query, w_key, w_value, w_out, jnp.swapaxes(key_a, 1, 2), key_b,
      jnp.swapaxes(value_a, 1, 2), value_b, cotangent)
    grad_a = jnp.einsum("psd,ptsr->tdr", sn_all.astype(F32), low_total, precision=HIGH)
    grad_b = jnp.einsum("ptsr,ptsc->trc", low_all, ks_all, preferred_element_type=F32)
    return (grad_a[None], grad_b[None])


def solution(mesh):
    placed = (
        P("dp", None, None),
        P("section", "dp", None, None),
        P("section", None),
        P("section", None, "mp"),
        P("section", None, "mp"),
        P("section", None, "mp"),
        P("section", "mp", None),
        P("section", None, None),
        P("section", None, "mp"),
        P("section", None, None),
        P("section", None, "mp"),
        P("dp", None, None),
    )
    return jax.shard_map(
        functools.partial(local, mesh.shape["dp"], mesh.shape["section"], mesh.shape["mp"]),
        mesh=mesh,
        in_specs=placed,
        out_specs=(P("section", None, None, None), P("section", None, None, "mp")),
        check_vma=False,
    )
```
